32 devices in a mesh: fam: 2 (over x), tm: 8 (over z, y), chan: 2 (over core).
Axes of the slice: x: 2, y: 2, z: 4, core: 2. Of those that a mesh axis runs over, the one named last changes fastest.
Arguments:
- records: float32 [3072, 4096], P(('fam', 'tm', 'chan')), parts along dimension 0, may hold values from -6 to 6
- row_dest: int32 [3072], P(('fam', 'tm', 'chan')), parts along dimension 0, may hold values from -1 to 7, as said below
- row_chan: int32 [3072], P(('fam', 'tm', 'chan')), parts along dimension 0, may hold values from 0 to 47, as said below
- row_len: int32 [3072], P(('fam', 'tm', 'chan')), parts along dimension 0, may hold values from 2048 to 4096
- templates: float32 [64, 16, 256], P(('fam', 'tm'), 'chan'), parts along dimension 0, may hold values from -6 to 6
- tmpl_chan: int32 [64, 16], P(('fam', 'tm'), 'chan'), parts along dimension 0, may hold values from 0 to 47
- tmpl_off: int32 [64, 16], P(('fam', 'tm'), 'chan'), parts along dimension 0, may hold values from 0 to 255
Outputs:
- detection: float32 [16, 4, 4, 3584], P(('fam', 'tm'), None, None, 'chan'), parts along dimension 0
The draws below stay inside these ranges and needn't reach their ends.
There are 2 independent parts, one for each index of `fam`. The reference program is written for one: setup_inputs(seed, part) draws one part's arguments, and reference() takes and returns one part's arrays. A program takes and returns all parts, laid end to end along the dimension named above; each array names one. Nothing has to cross between parts.
Inputs may be any that keep to these rules, and one draw needn't show every extreme that they name: `row_dest`: within the slots of the owners in one channel half, every pair of a time segment and a channel appears exactly once; one owner holds at most 12 rows of one time segment, and some owner holds exactly 12 of each. `row_chan`: 0 on empty slots.
All inputs are finite; a program needn't handle non-finite values.
Results may differ from the reference program's by a relative error of at most 0.0003.
Values sent between devices are 32-bit elements; how exact they have to be, the bound alone decides.
A program may use at most 128 MiB of HBM per device.

```python
import jax
import jax.numpy as jnp
from jax import lax

SAMPLES = 4096
TLEN = 256
TCH = 16
MAXOFF = 256
STOPS = 4
CH_DEV = 48
SLOTS = 96
OWN_ROWS = 1536
NT_DEV = 4
NTEMPL = 32
LAGS = 3584
N_TM = 8
N_CHAN = 2


def routing_tables(key):
    capacity = 2 * CH_DEV // N_TM
    busy_count = N_TM // 4
    busy_slots = busy_count * capacity
    spare_count = CH_DEV - busy_slots

    def one_half(half_key):
        order = jax.random.permutation(jax.random.fold_in(half_key, 1), N_TM)
        ranking = jnp.argsort(order)

        def one_segment(segment_key):
            channels = jax.random.permutation(jax.random.fold_in(segment_key, 1), CH_DEV).astype(jnp.int32)
            picks = jax.random.permutation(jax.random.fold_in(segment_key, 2), (N_TM - busy_count) * capacity)[:spare_count]
            table = jnp.full((N_TM * capacity,), -1, jnp.int32)
            table = table.at[jnp.arange(busy_slots)].set(channels[:busy_slots])
            table = table.at[busy_slots + picks].set(channels[busy_slots:])
            return table.reshape(N_TM, capacity)[ranking]
        segment_keys = jax.vmap(lambda number: jax.random.fold_in(half_key, number + 7))(jnp.arange(N_TM))
        return jax.vmap(one_segment)(segment_keys)
    half_keys = jax.vmap(lambda number: jax.random.fold_in(key, number + 101))(jnp.arange(N_CHAN))
    tables = jax.vmap(one_half)(half_keys)
    tables = jnp.transpose(tables, (2, 0, 1, 3)).reshape(N_TM * N_CHAN, 2 * CH_DEV)
    segment_ids = jnp.broadcast_to(jnp.arange(N_TM, dtype=jnp.int32)[:, None], (N_TM, capacity)).reshape(-1)
    dest_rows = jnp.where(tables >= 0, segment_ids[None, :], -1)
    shuffle_keys = jax.vmap(lambda number: jax.random.fold_in(key, number + 5003))(jnp.arange(N_TM * N_CHAN))
    shuffles = jax.vmap(lambda shuffle_key: jax.random.permutation(shuffle_key, 2 * CH_DEV))(shuffle_keys)
    chan_rows = jnp.take_along_axis(tables, shuffles, axis=1)
    dest_rows = jnp.take_along_axis(dest_rows, shuffles, axis=1)
    return (dest_rows.reshape(-1).astype(jnp.int32), jnp.maximum(chan_rows, 0).reshape(-1).astype(jnp.int32))


def draw_row_dest(key, part):
    return routing_tables(key)[0]


def draw_row_chan(key, part):
    return routing_tables(key)[1]


def draw_row_len(key, part):
    lengths = jax.random.randint(jax.random.fold_in(key, 31), (OWN_ROWS,), SAMPLES // 2, SAMPLES + 1)
    full_spot = jax.random.randint(jax.random.fold_in(key, 32), (), 0, OWN_ROWS)
    return lengths.at[full_spot].set(SAMPLES).astype(jnp.int32)


def place_ends(entries, rng, low, largest):
    index_at = [jax.random.randint(jax.random.fold_in(rng, axis), (), 0, length) for axis, length in enumerate(entries.shape)]
    widest = entries.shape.index(max(entries.shape))
    next_to = index_at[:widest] + [(index_at[widest] + 1) % entries.shape[widest]] + index_at[widest + 1:]
    return entries.at[tuple(index_at)].set(low).at[tuple(next_to)].set(largest)


def block_scale(rng, shape, shards, least, largest):
    def one(position, shards_of):
        heights = jax.random.uniform(jax.random.fold_in(jax.random.fold_in(rng, 6), position), (shards_of,), jnp.float32, least / len(shards), largest / len(shards))
        return jnp.repeat(jnp.exp(heights), shape[position] // shards_of).reshape((-1,) + (1,) * (len(shape) - position - 1))

    factor_of = one(*shards[0])
    for cut in shards[1:]:
        factor_of = factor_of * one(*cut)
    return factor_of


def gaussian(key, extent, deviation, reach, shards=(), held_as=jnp.bfloat16):
    result = deviation * jax.random.normal(key, extent, jnp.float32)
    if shards:
        result = result * block_scale(key, extent, shards, -0.22, 0.18)
    return jnp.clip(result, -reach, reach).astype(held_as)


def setup_inputs(seed: int = 0, part: int = 0) -> dict:
    arg_keys = jax.random.split(jax.random.key(seed), 8)
    part_splits = jax.random.split(jax.random.fold_in(arg_keys[7], part), 8)
    return {
        "records": gaussian(part_splits[0], (OWN_ROWS, SAMPLES), 1.0, 6.0, ((0, 16),), jnp.float32),
        "row_dest": draw_row_dest(jax.random.fold_in(jax.random.fold_in(arg_keys[7], part), 71), part),
        "row_chan": draw_row_chan(jax.random.fold_in(jax.random.fold_in(arg_keys[7], part), 71), part),
        "row_len": draw_row_len(jax.random.fold_in(jax.random.fold_in(arg_keys[7], part), 71), part),
        "templates": gaussian(part_splits[4], (NTEMPL, TCH, TLEN), 1.0, 6.0, ((0, 8), (1, 2)), jnp.float32),
        "tmpl_chan": place_ends(jax.random.randint(part_splits[5], (NTEMPL, TCH), 0, CH_DEV), jax.random.fold_in(part_splits[5], 1), 0, CH_DEV - 1).astype(jnp.int32),
        "tmpl_off": place_ends(jax.random.randint(part_splits[6], (NTEMPL, TCH), 0, MAXOFF), jax.random.fold_in(part_splits[6], 1), 0, MAXOFF - 1).astype(jnp.int32),
    }


FLOOR_SHARE = 0.25
TEMPLATE_EPS = 1e-06

def normalized(template_rows):
    centred = template_rows - lax.optimization_barrier(jnp.mean(template_rows, axis=-1, keepdims=True))
    energy = lax.optimization_barrier(jnp.sum(centred * centred, axis=-1, keepdims=True))
    return centred / jnp.sqrt(energy + TLEN * TEMPLATE_EPS)

def reference(records, row_dest, row_chan, row_len, templates, tmpl_chan, tmpl_off):
    positions = jnp.arange(SAMPLES, dtype=jnp.int32)
    masked = jnp.where(positions[None, :] < row_len[:, None], records, jnp.zeros_like(records))
    owner_half = (jnp.arange(OWN_ROWS, dtype=jnp.int32) // SLOTS % N_CHAN).astype(jnp.int32)
    target = jnp.where(row_dest >= 0, row_dest, N_TM).astype(jnp.int32)
    waveform = jnp.zeros((N_TM + 1, N_CHAN, CH_DEV, SAMPLES), records.dtype)
    waveform = waveform.at[target, owner_half, row_chan.astype(jnp.int32)].set(masked)[:N_TM]
    span_count = SAMPLES - TLEN
    zero_col = jnp.zeros(waveform.shape[:-1] + (1,), waveform.dtype)
    run_sum = jnp.concatenate([zero_col, jnp.cumsum(waveform, axis=-1)], axis=-1)
    run_sq = jnp.concatenate([zero_col, jnp.cumsum(waveform * waveform, axis=-1)], axis=-1)
    win_sum = run_sum[..., TLEN:TLEN + span_count] - run_sum[..., :span_count]
    win_sq = run_sq[..., TLEN:TLEN + span_count] - run_sq[..., :span_count]
    variance = win_sq - win_sum * win_sum / TLEN
    inv_sigma = 1.0 / jnp.sqrt(jnp.maximum(variance, FLOOR_SHARE * TLEN))
    spectra = jnp.fft.rfft(waveform, axis=-1)
    unit = normalized(templates)
    unit_spec = jnp.conj(jnp.fft.rfft(unit, n=SAMPLES, axis=-1))
    per_half = TCH // N_CHAN
    half_of = (jnp.arange(TCH, dtype=jnp.int32) // per_half).astype(jnp.int32)
    stack_gain = jnp.sqrt(1.0 * TLEN * TCH) / TCH

    def window_cut(row_corr, row_scale, offset):
        first = lax.dynamic_slice_in_dim(row_corr, offset, LAGS)
        second = lax.dynamic_slice_in_dim(row_scale, offset, LAGS)
        return first * second

    def one_segment(segment_index):
        segment_spec = spectra[segment_index]
        segment_scale = inv_sigma[segment_index]
        results = []
        for stop_index in range(STOPS):
            anchor = ((segment_index - stop_index) % N_TM).astype(jnp.int32)
            block_spec = lax.dynamic_slice_in_dim(unit_spec, anchor * NT_DEV, NT_DEV, 0)
            block_chan = lax.dynamic_slice_in_dim(tmpl_chan, anchor * NT_DEV, NT_DEV, 0)
            block_off = lax.dynamic_slice_in_dim(tmpl_off, anchor * NT_DEV, NT_DEV, 0)
            data_spec = segment_spec[half_of[None, :], block_chan]
            full_corr = jnp.fft.irfft(block_spec * data_spec, n=SAMPLES, axis=-1)
            scales = segment_scale[half_of[None, :], block_chan]
            ratios = jax.vmap(jax.vmap(window_cut))(full_corr, scales, block_off)
            results.append(stack_gain * lax.optimization_barrier(jnp.sum(ratios, axis=1)))
        return jnp.stack(results)
    return lax.map(one_segment, jnp.arange(N_TM, dtype=jnp.int32))
```

```python
import functools
import math

import jax
import jax.numpy as jnp
from jax import lax
from jax.experimental import pallas as pl
from jax.experimental.pallas import tpu as pltpu
from jax.sharding import PartitionSpec as P

MAXOFF = 256
STOPS = 4
FLOOR_SHARE = 0.25
TEMPLATE_EPS = 1e-06
LANES = 128


def flat_shift(x, by):
    rows = x.shape[-2]
    if by == LANES:
        return pltpu.roll(x, rows - 1, x.ndim - 2)
    lane = lax.broadcasted_iota(jnp.int32, x.shape, x.ndim - 1)
    moved = pltpu.roll(x, LANES - by, x.ndim - 1)
    below = pltpu.roll(moved, rows - 1, x.ndim - 2)
    return jnp.where(lane < LANES - by, moved, below)


def window_total(x, taps):
    span = 1
    while span < taps:
        x = x + flat_shift(x, span)
        span *= 2
    return x


def split(x):
    hi = x.astype(jnp.bfloat16)
    lo = (x - hi.astype(jnp.float32)).astype(jnp.bfloat16)
    return hi, lo


def correlate_kernel(
    gain, half_taps, chan_slot, pair_chan, pair_off, rows_ref, tmpl_ref, out_ref, unit_ref, win_ref, scale_ref
):
    pair_count, taps = tmpl_ref.shape
    channel_count = scale_ref.shape[0]
    blocks = rows_ref.shape[1]
    out_blocks = out_ref.shape[1]

    raw = tmpl_ref[...]
    centred = raw - jnp.mean(raw, axis=-1, keepdims=True)
    energy = jnp.sum(centred * centred, axis=-1, keepdims=True)
    unit_ref[...] = centred / jnp.sqrt(energy + taps * TEMPLATE_EPS)

    def one_channel(channel):
        x = rows_ref[chan_slot[channel]]
        win_sum = window_total(x, taps)
        win_sq = window_total(x * x, taps)
        variance = win_sq - win_sum * win_sum / taps
        scale_ref[channel] = gain / jnp.sqrt(jnp.maximum(variance, FLOOR_SHARE * taps))
        hi, lo = split(jnp.concatenate([x, pltpu.roll(x, blocks - 1, 0)], axis=1))
        win_ref[channel, :blocks] = hi
        win_ref[channel, blocks:] = lo

    def channel_group(group, carry):
        for j in range(4):
            one_channel(group * 4 + j)
        return carry

    lax.fori_loop(0, channel_count // 4, channel_group, 0)

    u_pos = lax.broadcasted_iota(jnp.int32, (LANES, LANES), 0)
    r_pos = lax.broadcasted_iota(jnp.int32, (LANES, LANES), 1)
    lower = u_pos >= r_pos
    lane = lax.broadcasted_iota(jnp.int32, (blocks, LANES), 1)
    none = jnp.zeros((LANES, LANES), jnp.bfloat16)

    def toeplitz(part):
        around, full = part[:, :LANES], part[:, LANES:]
        zero = jnp.zeros_like(around)
        top = jnp.concatenate([jnp.where(lower, around, zero).astype(jnp.bfloat16), none], axis=1)
        bottom = jnp.concatenate(
            [full.astype(jnp.bfloat16), jnp.where(lower, zero, around).astype(jnp.bfloat16)], axis=1
        )
        return jnp.concatenate([top, bottom], axis=0)

    def one_pair(pair):
        row = jnp.broadcast_to(unit_ref[pl.ds(pair, 1), :], (LANES, taps))
        table = pltpu.roll(row, 0, 1, stride=1, stride_axis=0)
        hi = table.astype(jnp.bfloat16).astype(jnp.float32)
        lo = table - hi
        channel = pair_chan[pair]
        windows = win_ref[channel]
        first = jnp.dot(windows, toeplitz(hi), preferred_element_type=jnp.float32)
        second = jnp.dot(windows[:blocks], toeplitz(lo), preferred_element_type=jnp.float32)
        both = first[:blocks] + first[blocks:] + second
        corr = both[:, :LANES] + pltpu.roll(both[:, LANES:], blocks - 1, 0)
        ratio = corr * scale_ref[channel]
        offset = pair_off[pair]
        low = lax.rem(offset, LANES)
        high = offset // LANES
        moved = pltpu.roll(ratio, lax.rem(LANES - low, LANES), 1)
        below = pltpu.roll(moved, blocks - 1, 0)
        below2 = pltpu.roll(moved, blocks - 2, 0)
        far = high > 0
        return jnp.where(lane < LANES - low, jnp.where(far, below, moved), jnp.where(far, below2, below))

    def one_template(template, carry):
        total = one_pair(template * half_taps)
        for i in range(1, half_taps):
            total = total + one_pair(template * half_taps + i)
        out_ref[template] = total[:out_blocks]
        return carry

    lax.fori_loop(0, out_ref.shape[0], one_template, 0)


def local(records, row_dest, row_chan, row_len, templates, tmpl_chan, tmpl_off):
    slot_count, sample_count = records.shape
    loop_size = lax.axis_size("tm")
    half_count = lax.axis_size("chan")
    capacity = slot_count // loop_size
    template_count, half_taps, tap_count = templates.shape
    assert tap_count == 2 * LANES
    blocks = sample_count // LANES
    lag_count = sample_count - tap_count - MAXOFF
    out_blocks = lag_count // LANES
    channel_count = slot_count // 2

    positions = lax.broadcasted_iota(jnp.int32, records.shape, 1)
    masked = jnp.where(positions < row_len[:, None], records, jnp.zeros_like(records))
    masked = masked.reshape(slot_count, blocks, LANES)
    slot_ids = jnp.arange(slot_count, dtype=jnp.int32)
    earlier = (row_dest[:, None] == row_dest[None, :]) & (slot_ids[None, :] < slot_ids[:, None])
    rank_within = jnp.sum(earlier.astype(jnp.int32), axis=1)
    target = jnp.where(row_dest >= 0, row_dest * capacity + rank_within, slot_count)
    outgoing = jnp.zeros_like(masked).at[target].set(masked, mode="drop")
    outgoing_ids = jnp.sum(
        jnp.where(target[None, :] == slot_ids[:, None], row_chan[None, :] + 1, 0), axis=1
    ) - 1
    arrived = lax.all_to_all(outgoing, "tm", split_axis=0, concat_axis=0, tiled=True)
    arrived_ids = lax.all_to_all(outgoing_ids, "tm", split_axis=0, concat_axis=0, tiled=True)

    extra = jnp.stack([tmpl_chan.reshape(-1), tmpl_off.reshape(-1)], axis=1).astype(jnp.float32)
    block = jnp.concatenate(
        [templates.reshape(-1, tap_count), jnp.pad(extra, ((0, 0), (0, LANES - 2)))], axis=1
    )
    visits = [block] + [
        lax.ppermute(block, "tm", [(i, (i + by) % loop_size) for i in range(loop_size)])
        for by in range(1, STOPS)
    ]
    visits = jnp.concatenate(visits, axis=0)
    taps_back = jnp.roll(visits[:, :tap_count][:, ::-1], 1, axis=1)
    pair_chan = visits[:, tap_count].astype(jnp.int32)
    pair_off = visits[:, tap_count + 1].astype(jnp.int32)
    channels = jnp.arange(channel_count, dtype=jnp.int32)
    chan_slot = jnp.sum(
        jnp.where(arrived_ids[None, :] == channels[:, None], slot_ids[None, :], 0), axis=1
    )

    pair_count = visits.shape[0]
    gain = math.sqrt(tap_count * half_taps * half_count) / (half_taps * half_count)
    smem = pl.BlockSpec(memory_space=pltpu.SMEM)
    vmem = pl.BlockSpec(memory_space=pltpu.VMEM)
    partial = pl.pallas_call(
        functools.partial(correlate_kernel, gain, half_taps),
        out_shape=jax.ShapeDtypeStruct((STOPS * template_count, out_blocks, LANES), jnp.float32),
        in_specs=[smem, smem, smem, vmem, vmem],
        out_specs=vmem,
        scratch_shapes=[
            pltpu.VMEM((pair_count, tap_count), jnp.float32),
            pltpu.VMEM((channel_count, 2 * blocks, tap_count), jnp.bfloat16),
            pltpu.VMEM((channel_count, blocks, LANES), jnp.float32),
        ],
        compiler_params=pltpu.CompilerParams(vmem_limit_bytes=40 * 2**20),
        cost_estimate=pl.CostEstimate(
            flops=2 * 3 * pair_count * blocks * tap_count * tap_count,
            bytes_accessed=8 * slot_count * sample_count,
            transcendentals=0,
        ),
    )(chan_slot, pair_chan, pair_off, arrived, taps_back)

    half = lax.axis_index("chan")
    share = out_blocks // half_count
    keep = lax.dynamic_slice_in_dim(partial, half * share, share, 1)
    send = lax.dynamic_slice_in_dim(partial, (1 - half) * share, share, 1)
    got = lax.ppermute(send, "chan", [(0, 1), (1, 0)])
    return (keep + got).reshape(1, STOPS, template_count, share * LANES)


def solution(mesh):
    in_specs = (
        P(("fam", "tm", "chan"), None),
        P(("fam", "tm", "chan")),
        P(("fam", "tm", "chan")),
        P(("fam", "tm", "chan")),
        P(("fam", "tm"), "chan", None),
        P(("fam", "tm"), "chan"),
        P(("fam", "tm"), "chan"),
    )
    out_specs = P(("fam", "tm"), None, None, "chan")
    return jax.shard_map(local, mesh=mesh, in_specs=in_specs, out_specs=out_specs, check_vma=False)
```

```python
import functools
import math

import jax
import jax.numpy as jnp
from jax import lax
from jax.experimental import pallas as pl
from jax.experimental.pallas import tpu as pltpu
from jax.sharding import PartitionSpec as P

MAXOFF = 256
STOPS = 4
FLOOR_SHARE = 0.25
TEMPLATE_EPS = 1e-06
LANES = 128


def flat_shift(x, by):
    rows = x.shape[-2]
    if by == LANES:
        return pltpu.roll(x, rows - 1, x.ndim - 2)
    lane = lax.broadcasted_iota(jnp.int32, x.shape, x.ndim - 1)
    moved = pltpu.roll(x, LANES - by, x.ndim - 1)
    below = pltpu.roll(moved, rows - 1, x.ndim - 2)
    return jnp.where(lane < LANES - by, moved, below)


def window_total(x, taps):
    span = 1
    while span < taps:
        x = x + flat_shift(x, span)
        span *= 2
    return x


def split(x):
    hi = x.astype(jnp.bfloat16)
    lo = (x - hi.astype(jnp.float32)).astype(jnp.bfloat16)
    return hi, lo


def neighbour(axis, by):
    return lax.rem(lax.axis_index(axis) + by, lax.axis_size(axis))


def stack_kernel(
    gain, half_taps, capacity, src_slot, rows_ref, ids_ref, tmpl_ref, out_ref,
    send_buf, recv_buf, visit_buf, unit_ref, table_ref, win_ref, scale_ref, map_ref, map_smem, part_ref, other_ref,
    send_sem, recv_sem, tsend_sem, trecv_sem, csend_sem, crecv_sem, map_sem,
):
    peers = lax.axis_size("tm")
    me, half = lax.axis_index("tm"), lax.axis_index("chan")
    taps = unit_ref.shape[1]
    pair_rows = unit_ref.shape[0] // STOPS
    blocks = scale_ref.shape[1]
    share = out_ref.shape[1]

    barrier = pltpu.get_barrier_semaphore()

    def greet(k, carry):
        pl.semaphore_signal(
            barrier, inc=1, device_id={"tm": neighbour("tm", k)}, device_id_type=pl.DeviceIdType.MESH
        )
        return carry

    lax.fori_loop(1, peers, greet, 0)
    pl.semaphore_signal(barrier, inc=1, device_id={"chan": 1 - half}, device_id_type=pl.DeviceIdType.MESH)
    pl.semaphore_wait(barrier, peers)

    def visit_copy(by):
        return pltpu.make_async_remote_copy(
            src_ref=visit_buf.at[0],
            dst_ref=visit_buf.at[by],
            send_sem=tsend_sem.at[by],
            recv_sem=trecv_sem.at[by],
            device_id={"tm": neighbour("tm", by)},
            device_id_type=pl.DeviceIdType.MESH,
        )

    def rows_copy(k):
        return pltpu.make_async_remote_copy(
            src_ref=send_buf.at[k],
            dst_ref=recv_buf.at[k],
            send_sem=send_sem.at[k],
            recv_sem=recv_sem.at[k],
            device_id={"tm": neighbour("tm", k)},
            device_id_type=pl.DeviceIdType.MESH,
        )

    def pack(k, buf):
        dest = neighbour("tm", k)
        for r in range(capacity):
            buf[k, r * blocks:(r + 1) * blocks, :] = rows_ref[src_slot[dest * capacity + r]]
        buf[k, capacity * blocks:, :] = ids_ref[dest]

    visit_buf[0] = tmpl_ref[...]
    for by in range(1, STOPS):
        visit_copy(by).start()

    def send_block(k, carry):
        pack(k, send_buf)
        rows_copy(k).start()
        return carry

    lax.fori_loop(1, peers, send_block, 0)
    pack(0, recv_buf)

    u_pos = lax.broadcasted_iota(jnp.int32, (LANES, LANES), 0)
    r_pos = lax.broadcasted_iota(jnp.int32, (LANES, LANES), 1)
    lower = u_pos >= r_pos

    def put_table(pair, which, piece):
        around, full = piece[:, :LANES], piece[:, LANES:]
        zero = jnp.zeros_like(around)
        table_ref[pair, which, :LANES, :LANES] = jnp.where(lower, around, zero).astype(jnp.bfloat16)
        table_ref[pair, which, :LANES, LANES:] = zero.astype(jnp.bfloat16)
        table_ref[pair, which, LANES:, :LANES] = full.astype(jnp.bfloat16)
        table_ref[pair, which, LANES:, LANES:] = jnp.where(lower, zero, around).astype(jnp.bfloat16)

    def put_pair(pair):
        row = jnp.broadcast_to(unit_ref[pl.ds(pair, 1), :], (LANES, taps))
        table = pltpu.roll(row, 0, 1, stride=1, stride_axis=0)
        hi = table.astype(jnp.bfloat16).astype(jnp.float32)
        put_table(pair, 0, hi)
        put_table(pair, 1, table - hi)

    for by in range(STOPS):
        if by > 0:
            visit_copy(by).wait_recv()
        raw = visit_buf[by, :pair_rows, :]
        centred = raw - jnp.mean(raw, axis=-1, keepdims=True)
        energy = jnp.sum(centred * centred, axis=-1, keepdims=True)
        unit_ref[by * pair_rows:(by + 1) * pair_rows, :] = centred / jnp.sqrt(energy + taps * TEMPLATE_EPS)

        def pair_group(group, carry, by=by):
            for j in range(2):
                put_pair(by * pair_rows + group * 2 + j)
            return carry

        lax.fori_loop(0, pair_rows // 2, pair_group, 0)

    unroll = 4 if capacity % 4 == 0 else 1

    def one_row(k, r):
        x = recv_buf[k, pl.ds(pl.multiple_of(r * blocks, 8), blocks), :]
        win_sum = window_total(x, taps)
        win_sq = window_total(x * x, taps)
        variance = win_sq - win_sum * win_sum / taps
        slot = k * capacity + r
        scale_ref[slot] = gain / jnp.sqrt(jnp.maximum(variance, FLOOR_SHARE * taps))
        hi, lo = split(jnp.concatenate([x, pltpu.roll(x, blocks - 1, 0)], axis=1))
        win_ref[slot, :blocks] = hi
        win_ref[slot, blocks:] = lo

    def rows_of(k):
        def group_of(group, carry):
            for j in range(unroll):
                one_row(k, group * unroll + j)
            return carry

        lax.fori_loop(0, capacity // unroll, group_of, 0)

    def arrive(k, carry):
        rows_copy(k).wait_recv()
        rows_of(k)
        return carry

    rows_of(0)
    lax.fori_loop(1, peers, arrive, 0)

    id_rows = recv_buf.shape[1] - capacity * blocks
    order = lax.broadcasted_iota(jnp.int32, (id_rows, LANES), 0)
    for by in range(STOPS):
        wanted = visit_buf[by, pair_rows:pair_rows + 1, :LANES]

        def find(k, found, wanted=wanted):
            held = recv_buf[k, capacity * blocks:, :]
            number = (order + k * capacity).astype(jnp.float32)
            return jnp.maximum(found, jnp.max(jnp.where(held == wanted, number, 0.0), axis=0, keepdims=True))

        found = lax.fori_loop(0, peers, find, jnp.zeros((1, LANES), jnp.float32))
        map_ref[by:by + 1, :] = jnp.clip(found.astype(jnp.int32), 0, peers * capacity - 1)
        map_ref[STOPS + by:STOPS + by + 1, :] = visit_buf[by, pair_rows + 1:pair_rows + 2, :LANES].astype(jnp.int32)
    map_copy = pltpu.make_async_copy(map_ref, map_smem, map_sem)
    map_copy.start()
    map_copy.wait()

    lane = lax.broadcasted_iota(jnp.int32, (blocks, LANES), 1)

    def one_pair(by, place):
        pair = by * pair_rows + place
        slot = jnp.clip(map_smem[by, place], 0, peers * capacity - 1)
        offset = map_smem[STOPS + by, place]
        windows = win_ref[slot]
        first = jnp.dot(windows, table_ref[pair, 0], preferred_element_type=jnp.float32)
        second = jnp.dot(windows[:blocks], table_ref[pair, 1], preferred_element_type=jnp.float32)
        both = first[:blocks] + first[blocks:] + second
        corr = both[:, :LANES] + pltpu.roll(both[:, LANES:], blocks - 1, 0)
        ratio = corr * scale_ref[slot]
        far = offset >= LANES
        low = jnp.where(far, offset - LANES, offset)
        moved = pltpu.roll(ratio, jnp.where(low == 0, 0, LANES - low), 1)
        below = pltpu.roll(moved, blocks - 1, 0)
        below2 = pltpu.roll(moved, blocks - 2, 0)
        return jnp.where(lane < LANES - low, jnp.where(far, below, moved), jnp.where(far, below2, below))

    for by in range(STOPS):
        def one_template(template, carry, by=by):
            total = one_pair(by, template * half_taps)
            for i in range(1, half_taps):
                total = total + one_pair(by, template * half_taps + i)
            place = by * (pair_rows // half_taps) + template
            part_ref[0, place] = total[:share]
            part_ref[1, place] = total[share:2 * share]
            return carry

        lax.fori_loop(0, pair_rows // half_taps, one_template, 0)

    swap = pltpu.make_async_remote_copy(
        src_ref=part_ref.at[1 - half],
        dst_ref=other_ref,
        send_sem=csend_sem,
        recv_sem=crecv_sem,
        device_id={"chan": 1 - half},
        device_id_type=pl.DeviceIdType.MESH,
    )
    swap.start()
    for by in range(1, STOPS):
        visit_copy(by).wait_send()

    def sent(k, carry):
        rows_copy(k).wait_send()
        return carry

    lax.fori_loop(1, peers, sent, 0)
    swap.wait()
    out_ref[...] = part_ref[half] + other_ref[...]


def local(records, row_dest, row_chan, row_len, templates, tmpl_chan, tmpl_off):
    slot_count, sample_count = records.shape
    peers = lax.axis_size("tm")
    half_count = lax.axis_size("chan")
    capacity = slot_count // peers
    template_count, half_taps, tap_count = templates.shape
    assert tap_count == 2 * LANES and half_count == 2
    blocks = sample_count // LANES
    lag_count = sample_count - tap_count - MAXOFF
    share = lag_count // LANES // half_count

    positions = lax.broadcasted_iota(jnp.int32, records.shape, 1)
    masked = jnp.where(positions < row_len[:, None], records, jnp.zeros_like(records))
    masked = masked.reshape(slot_count, blocks, LANES)
    slot_ids = jnp.arange(slot_count, dtype=jnp.int32)
    earlier = (row_dest[:, None] == row_dest[None, :]) & (slot_ids[None, :] < slot_ids[:, None])
    rank_within = jnp.sum(earlier.astype(jnp.int32), axis=1)
    target = jnp.where(row_dest >= 0, row_dest * capacity + rank_within, slot_count)
    here = target[None, :] == slot_ids[:, None]
    src_slot = jnp.sum(jnp.where(here, slot_ids[None, :], 0), axis=1)
    ids = jnp.sum(jnp.where(here, row_chan[None, :] + 1, 0), axis=1) - 1
    id_rows = -(-capacity // 8) * 8
    ids = jnp.pad(ids.reshape(peers, capacity), ((0, 0), (0, id_rows - capacity)), constant_values=-1)
    ids = jnp.broadcast_to(ids.astype(jnp.float32)[:, :, None], (peers, id_rows, LANES))

    pair_rows = template_count * half_taps
    taps_back = jnp.roll(templates.reshape(pair_rows, tap_count)[:, ::-1], 1, axis=1)
    extra = jnp.stack([tmpl_chan.reshape(-1), tmpl_off.reshape(-1)]).astype(jnp.float32)
    extra = jnp.pad(extra, ((0, 6), (0, tap_count - pair_rows)))
    block = jnp.concatenate([taps_back, extra], axis=0)

    pair_count = STOPS * pair_rows
    gain = math.sqrt(tap_count * half_taps * half_count) / (half_taps * half_count)
    smem = pl.BlockSpec(memory_space=pltpu.SMEM)
    vmem = pl.BlockSpec(memory_space=pltpu.VMEM)
    block_rows = capacity * blocks + id_rows
    out = pl.pallas_call(
        functools.partial(stack_kernel, gain, half_taps, capacity),
        out_shape=jax.ShapeDtypeStruct((STOPS * template_count, share, LANES), jnp.float32),
        in_specs=[smem, vmem, vmem, vmem],
        out_specs=vmem,
        scratch_shapes=[
            pltpu.VMEM((peers, block_rows, LANES), jnp.float32),
            pltpu.VMEM((peers, block_rows, LANES), jnp.float32),
            pltpu.VMEM((STOPS,) + block.shape, jnp.float32),
            pltpu.VMEM((pair_count, tap_count), jnp.float32),
            pltpu.VMEM((pair_count, 2, tap_count, tap_count), jnp.bfloat16),
            pltpu.VMEM((slot_count, 2 * blocks, tap_count), jnp.bfloat16),
            pltpu.VMEM((slot_count, blocks, LANES), jnp.float32),
            pltpu.VMEM((2 * STOPS, LANES), jnp.int32),
            pltpu.SMEM((2 * STOPS, LANES), jnp.int32),
            pltpu.VMEM((2, STOPS * template_count, share, LANES), jnp.float32),
            pltpu.VMEM((STOPS * template_count, share, LANES), jnp.float32),
            pltpu.SemaphoreType.DMA((peers,)),
            pltpu.SemaphoreType.DMA((peers,)),
            pltpu.SemaphoreType.DMA((STOPS,)),
            pltpu.SemaphoreType.DMA((STOPS,)),
            pltpu.SemaphoreType.DMA,
            pltpu.SemaphoreType.DMA,
            pltpu.SemaphoreType.DMA,
        ],
        compiler_params=pltpu.CompilerParams(
            vmem_limit_bytes=56 * 2**20, collective_id=0, has_side_effects=True
        ),
        cost_estimate=pl.CostEstimate(
            flops=2 * 3 * pair_count * blocks * tap_count * tap_count,
            bytes_accessed=8 * slot_count * sample_count,
            transcendentals=0,
        ),
    )(src_slot, masked, ids, block)
    return out.reshape(1, STOPS, template_count, share * LANES)


def solution(mesh):
    in_specs = (
        P(("fam", "tm", "chan"), None),
        P(("fam", "tm", "chan")),
        P(("fam", "tm", "chan")),
        P(("fam", "tm", "chan")),
        P(("fam", "tm"), "chan", None),
        P(("fam", "tm"), "chan"),
        P(("fam", "tm"), "chan"),
    )
    out_specs = P(("fam", "tm"), None, None, "chan")
    return jax.shard_map(local, mesh=mesh, in_specs=in_specs, out_specs=out_specs, check_vma=False)
```

```python
import functools
import math

import jax
import jax.numpy as jnp
from jax import lax
from jax.experimental import pallas as pl
from jax.experimental.pallas import tpu as pltpu
from jax.sharding import PartitionSpec as P

MAXOFF = 256
STOPS = 4
FLOOR_SHARE = 0.25
TEMPLATE_EPS = 1e-06
LANES = 128


def flat_shift(x, by):
    rows = x.shape[-2]
    if by == LANES:
        return pltpu.roll(x, rows - 1, x.ndim - 2)
    lane = lax.broadcasted_iota(jnp.int32, x.shape, x.ndim - 1)
    moved = pltpu.roll(x, LANES - by, x.ndim - 1)
    below = pltpu.roll(moved, rows - 1, x.ndim - 2)
    return jnp.where(lane < LANES - by, moved, below)


def window_total(x, taps):
    span = 1
    while span < taps:
        x = x + flat_shift(x, span)
        span *= 2
    return x


def split(x):
    hi = x.astype(jnp.bfloat16)
    lo = (x - hi.astype(jnp.float32)).astype(jnp.bfloat16)
    return hi, lo


def neighbour(axis, by):
    return lax.rem(lax.axis_index(axis) + by, lax.axis_size(axis))


def stack_kernel(
    gain, half_taps, capacity, src_slot, row_len, records_ref, ids_ref, tmpl_ref, out_ref,
    spread_ref, rows_ref, id_ref, send_buf, recv_buf, visit_buf, unit_ref, table_ref, win_ref, scale_ref, map_ref, map_smem, part_ref, other_ref,
    send_sem, recv_sem, tsend_sem, trecv_sem, csend_sem, crecv_sem, map_sem,
):
    peers = lax.axis_size("tm")
    me, half = lax.axis_index("tm"), lax.axis_index("chan")
    taps = unit_ref.shape[1]
    pair_rows = unit_ref.shape[0] // STOPS
    blocks = scale_ref.shape[1]
    share = other_ref.shape[1]
    position = LANES * lax.broadcasted_iota(jnp.int32, (blocks, LANES), 0) + lax.broadcasted_iota(
        jnp.int32, (blocks, LANES), 1
    )

    def by_distance(j):
        step = (j + 1) // 2
        return peers // 2 + step * (1 - 2 * lax.rem(j, 2))

    barrier = pltpu.get_barrier_semaphore()

    def greet(k, carry):
        pl.semaphore_signal(
            barrier, inc=1, device_id={"tm": neighbour("tm", k)}, device_id_type=pl.DeviceIdType.MESH
        )
        return carry

    lax.fori_loop(1, peers, greet, 0)
    pl.semaphore_signal(barrier, inc=1, device_id={"chan": 1 - half}, device_id_type=pl.DeviceIdType.MESH)

    def spread(group, carry):
        rows = records_ref[pl.ds(pl.multiple_of(group * 8, 8), 8), :]
        for b in range(blocks):
            spread_ref[pl.ds(b, 8, stride=blocks), :] = rows[:, b * LANES:(b + 1) * LANES]
        for r in range(8):
            rows_ref[group * 8 + r] = spread_ref[r * blocks:(r + 1) * blocks, :]
        return carry

    lax.fori_loop(0, records_ref.shape[0] // 8, spread, 0)
    pl.semaphore_wait(barrier, peers)

    def visit_copy(by):
        return pltpu.make_async_remote_copy(
            src_ref=visit_buf.at[0],
            dst_ref=visit_buf.at[by],
            send_sem=tsend_sem.at[by],
            recv_sem=trecv_sem.at[by],
            device_id={"tm": neighbour("tm", by)},
            device_id_type=pl.DeviceIdType.MESH,
        )

    def rows_copy(k):
        return pltpu.make_async_remote_copy(
            src_ref=send_buf.at[k],
            dst_ref=recv_buf.at[k],
            send_sem=send_sem.at[k],
            recv_sem=recv_sem.at[k],
            device_id={"tm": neighbour("tm", k)},
            device_id_type=pl.DeviceIdType.MESH,
        )

    def pack(k, buf):
        dest = neighbour("tm", k)
        for r in range(capacity):
            src = src_slot[dest * capacity + r]
            buf[k, r * blocks:(r + 1) * blocks, :] = jnp.where(position < row_len[src], rows_ref[src], 0.0)
        buf[k, capacity * blocks:, :] = ids_ref[dest]

    visit_buf[0] = tmpl_ref[...]
    for by in range(1, STOPS):
        visit_copy(by).start()

    def send_block(j, carry):
        k = by_distance(j)
        pack(k, send_buf)
        rows_copy(k).start()
        return carry

    lax.fori_loop(0, peers - 1, send_block, 0)
    pack(0, recv_buf)

    u_pos = lax.broadcasted_iota(jnp.int32, (LANES, LANES), 0)
    r_pos = lax.broadcasted_iota(jnp.int32, (LANES, LANES), 1)
    lower = u_pos >= r_pos

    def put_table(pair, which, piece):
        around, full = piece[:, :LANES], piece[:, LANES:]
        zero = jnp.zeros_like(around)
        table_ref[pair, which, :LANES, :LANES] = jnp.where(lower, around, zero).astype(jnp.bfloat16)
        table_ref[pair, which, :LANES, LANES:] = zero.astype(jnp.bfloat16)
        table_ref[pair, which, LANES:, :LANES] = full.astype(jnp.bfloat16)
        table_ref[pair, which, LANES:, LANES:] = jnp.where(lower, zero, around).astype(jnp.bfloat16)

    def put_pair(pair):
        row = jnp.broadcast_to(unit_ref[pl.ds(pair, 1), :], (LANES, taps))
        table = pltpu.roll(row, 0, 1, stride=1, stride_axis=0)
        hi = table.astype(jnp.bfloat16).astype(jnp.float32)
        put_table(pair, 0, hi)
        put_table(pair, 1, table - hi)

    for by in range(STOPS):
        if by > 0:
            visit_copy(by).wait_recv()
        raw = visit_buf[by, :pair_rows, :]
        centred = raw - jnp.mean(raw, axis=-1, keepdims=True)
        energy = jnp.sum(centred * centred, axis=-1, keepdims=True)
        unit_ref[by * pair_rows:(by + 1) * pair_rows, :] = centred / jnp.sqrt(energy + taps * TEMPLATE_EPS)

        def pair_group(group, carry, by=by):
            for j in range(2):
                put_pair(by * pair_rows + group * 2 + j)
            return carry

        lax.fori_loop(0, pair_rows // 2, pair_group, 0)

    unroll = 4 if capacity % 4 == 0 else 1

    def one_row(k, r):
        x = recv_buf[k, pl.ds(pl.multiple_of(r * blocks, 8), blocks), :]
        win_sum = window_total(x, taps)
        win_sq = window_total(x * x, taps)
        variance = win_sq - win_sum * win_sum / taps
        slot = k * capacity + r
        scale_ref[slot] = gain / jnp.sqrt(jnp.maximum(variance, FLOOR_SHARE * taps))
        hi, lo = split(jnp.concatenate([x, pltpu.roll(x, blocks - 1, 0)], axis=1))
        win_ref[slot, :blocks] = hi
        win_ref[slot, blocks:] = lo

    def rows_of(k):
        def group_of(group, carry):
            for j in range(unroll):
                one_row(k, group * unroll + j)
            return carry

        lax.fori_loop(0, capacity // unroll, group_of, 0)
        id_row = recv_buf[k, capacity * blocks:capacity * blocks + 1, :]
        id_ref[k] = jnp.transpose(jnp.broadcast_to(id_row, (LANES, LANES)))[:id_ref.shape[1]]

    def arrive(j, carry):
        k = by_distance(peers - 2 - j)
        rows_copy(k).wait_recv()
        rows_of(k)
        return carry

    rows_of(0)
    lax.fori_loop(0, peers - 1, arrive, 0)

    id_rows = id_ref.shape[1]
    order = lax.broadcasted_iota(jnp.int32, (id_rows, LANES), 0)
    for by in range(STOPS):
        wanted = visit_buf[by, pair_rows:pair_rows + 1, :LANES]

        def find(k, found, wanted=wanted):
            held = id_ref[k]
            number = (order + k * capacity).astype(jnp.float32)
            return jnp.maximum(found, jnp.max(jnp.where(held == wanted, number, 0.0), axis=0, keepdims=True))

        found = lax.fori_loop(0, peers, find, jnp.zeros((1, LANES), jnp.float32))
        map_ref[by:by + 1, :] = jnp.clip(found.astype(jnp.int32), 0, peers * capacity - 1)
        map_ref[STOPS + by:STOPS + by + 1, :] = visit_buf[by, pair_rows + 1:pair_rows + 2, :LANES].astype(jnp.int32)
    map_copy = pltpu.make_async_copy(map_ref, map_smem, map_sem)
    map_copy.start()
    map_copy.wait()

    lane = lax.broadcasted_iota(jnp.int32, (blocks, LANES), 1)

    def one_pair(by, place):
        pair = by * pair_rows + place
        slot = jnp.clip(map_smem[by, place], 0, peers * capacity - 1)
        offset = map_smem[STOPS + by, place]
        windows = win_ref[slot]
        first = jnp.dot(windows, table_ref[pair, 0], preferred_element_type=jnp.float32)
        second = jnp.dot(windows[:blocks], table_ref[pair, 1], preferred_element_type=jnp.float32)
        both = first[:blocks] + first[blocks:] + second
        corr = both[:, :LANES] + pltpu.roll(both[:, LANES:], blocks - 1, 0)
        ratio = corr * scale_ref[slot]
        far = offset >= LANES
        low = jnp.where(far, offset - LANES, offset)
        moved = pltpu.roll(ratio, jnp.where(low == 0, 0, LANES - low), 1)
        below = pltpu.roll(moved, blocks - 1, 0)
        below2 = pltpu.roll(moved, blocks - 2, 0)
        return jnp.where(lane < LANES - low, jnp.where(far, below, moved), jnp.where(far, below2, below))

    group_size = pair_rows // half_taps

    def swap(by):
        group = pl.ds(by * group_size, group_size)
        return pltpu.make_async_remote_copy(
            src_ref=part_ref.at[1 - half, group],
            dst_ref=other_ref.at[group],
            send_sem=csend_sem.at[by],
            recv_sem=crecv_sem.at[by],
            device_id={"chan": 1 - half},
            device_id_type=pl.DeviceIdType.MESH,
        )

    for by in range(STOPS):
        def one_template(template, carry, by=by):
            total = one_pair(by, template * half_taps)
            for i in range(1, half_taps):
                total = total + one_pair(by, template * half_taps + i)
            place = by * group_size + template
            part_ref[0, place] = total[:share]
            part_ref[1, place] = total[share:2 * share]
            return carry

        lax.fori_loop(0, group_size, one_template, 0)
        swap(by).start()

    for by in range(1, STOPS):
        visit_copy(by).wait_send()

    def sent(k, carry):
        rows_copy(k).wait_send()
        return carry

    lax.fori_loop(1, peers, sent, 0)
    for by in range(STOPS):
        swap(by).wait()
        group = pl.ds(by * group_size, group_size)
        stacks = part_ref[half, group] + other_ref[group]
        for b in range(share):
            out_ref[0, by, :, b * LANES:(b + 1) * LANES] = stacks[:, b, :]


def local(records, row_dest, row_chan, row_len, templates, tmpl_chan, tmpl_off):
    slot_count, sample_count = records.shape
    peers = lax.axis_size("tm")
    half_count = lax.axis_size("chan")
    capacity = slot_count // peers
    template_count, half_taps, tap_count = templates.shape
    assert tap_count == 2 * LANES and half_count == 2
    blocks = sample_count // LANES
    lag_count = sample_count - tap_count - MAXOFF
    share = lag_count // LANES // half_count

    slot_ids = jnp.arange(slot_count, dtype=jnp.int32)
    earlier = (row_dest[:, None] == row_dest[None, :]) & (slot_ids[None, :] < slot_ids[:, None])
    rank_within = jnp.sum(earlier.astype(jnp.int32), axis=1)
    target = jnp.where(row_dest >= 0, row_dest * capacity + rank_within, slot_count)
    here = target[None, :] == slot_ids[:, None]
    src_slot = jnp.sum(jnp.where(here, slot_ids[None, :], 0), axis=1)
    ids = jnp.sum(jnp.where(here, row_chan[None, :] + 1, 0), axis=1) - 1
    id_rows = -(-capacity // 8) * 8
    ids = jnp.pad(ids.reshape(peers, capacity), ((0, 0), (0, LANES - capacity)), constant_values=-1)
    ids = jnp.broadcast_to(ids.astype(jnp.float32)[:, None, :], (peers, 8, LANES))

    pair_rows = template_count * half_taps
    taps_back = jnp.roll(templates.reshape(pair_rows, tap_count)[:, ::-1], 1, axis=1)
    extra = jnp.stack([tmpl_chan.reshape(-1), tmpl_off.reshape(-1)]).astype(jnp.float32)
    extra = jnp.pad(extra, ((0, 6), (0, tap_count - pair_rows)))
    block = jnp.concatenate([taps_back, extra], axis=0)

    pair_count = STOPS * pair_rows
    gain = math.sqrt(tap_count * half_taps * half_count) / (half_taps * half_count)
    smem = pl.BlockSpec(memory_space=pltpu.SMEM)
    vmem = pl.BlockSpec(memory_space=pltpu.VMEM)
    block_rows = capacity * blocks + 8
    out = pl.pallas_call(
        functools.partial(stack_kernel, gain, half_taps, capacity),
        out_shape=jax.ShapeDtypeStruct((1, STOPS, template_count, share * LANES), jnp.float32),
        in_specs=[smem, smem, vmem, vmem, vmem],
        out_specs=vmem,
        scratch_shapes=[
            pltpu.VMEM((8 * blocks, LANES), jnp.float32),
            pltpu.VMEM((slot_count, blocks, LANES), jnp.float32),
            pltpu.VMEM((peers, id_rows, LANES), jnp.float32),
            pltpu.VMEM((peers, block_rows, LANES), jnp.float32),
            pltpu.VMEM((peers, block_rows, LANES), jnp.float32),
            pltpu.VMEM((STOPS,) + block.shape, jnp.float32),
            pltpu.VMEM((pair_count, tap_count), jnp.float32),
            pltpu.VMEM((pair_count, 2, tap_count, tap_count), jnp.bfloat16),
            pltpu.VMEM((slot_count, 2 * blocks, tap_count), jnp.bfloat16),
            pltpu.VMEM((slot_count, blocks, LANES), jnp.float32),
            pltpu.VMEM((2 * STOPS, LANES), jnp.int32),
            pltpu.SMEM((2 * STOPS, LANES), jnp.int32),
            pltpu.VMEM((2, STOPS * template_count, share, LANES), jnp.float32),
            pltpu.VMEM((STOPS * template_count, share, LANES), jnp.float32),
            pltpu.SemaphoreType.DMA((peers,)),
            pltpu.SemaphoreType.DMA((peers,)),
            pltpu.SemaphoreType.DMA((STOPS,)),
            pltpu.SemaphoreType.DMA((STOPS,)),
            pltpu.SemaphoreType.DMA((STOPS,)),
            pltpu.SemaphoreType.DMA((STOPS,)),
            pltpu.SemaphoreType.DMA,
        ],
        compiler_params=pltpu.CompilerParams(
            vmem_limit_bytes=56 * 2**20, collective_id=0, has_side_effects=True
        ),
        cost_estimate=pl.CostEstimate(
            flops=2 * 3 * pair_count * blocks * tap_count * tap_count,
            bytes_accessed=8 * slot_count * sample_count,
            transcendentals=0,
        ),
    )(src_slot, row_len, records, ids, block)
    return out


def solution(mesh):
    in_specs = (
        P(("fam", "tm", "chan"), None),
        P(("fam", "tm", "chan")),
        P(("fam", "tm", "chan")),
        P(("fam", "tm", "chan")),
        P(("fam", "tm"), "chan", None),
        P(("fam", "tm"), "chan"),
        P(("fam", "tm"), "chan"),
    )
    out_specs = P(("fam", "tm"), None, None, "chan")
    return jax.shard_map(local, mesh=mesh, in_specs=in_specs, out_specs=out_specs, check_vma=False)
```

```python
import functools
import math

import jax
import jax.numpy as jnp
from jax import lax
from jax.experimental import pallas as pl
from jax.experimental.pallas import tpu as pltpu
from jax.sharding import PartitionSpec as P

MAXOFF = 256
STOPS = 4
FLOOR_SHARE = 0.25
TEMPLATE_EPS = 1e-06
LANES = 128


def flat_shift(x, by):
    rows = x.shape[-2]
    if by == LANES:
        return pltpu.roll(x, rows - 1, x.ndim - 2)
    lane = lax.broadcasted_iota(jnp.int32, x.shape, x.ndim - 1)
    moved = pltpu.roll(x, LANES - by, x.ndim - 1)
    below = pltpu.roll(moved, rows - 1, x.ndim - 2)
    return jnp.where(lane < LANES - by, moved, below)


def window_total(x, taps):
    span = 1
    while span < taps:
        x = x + flat_shift(x, span)
        span *= 2
    return x


def split(x):
    hi = x.astype(jnp.bfloat16)
    lo = (x - hi.astype(jnp.float32)).astype(jnp.bfloat16)
    return hi, lo


def neighbour(axis, by):
    return lax.rem(lax.axis_index(axis) + by, lax.axis_size(axis))


def partner(k):
    me, peers = lax.axis_index("tm"), lax.axis_size("tm")
    if peers & (peers - 1):
        return lax.rem(peers + k - me, peers)
    other, bit = 0, 1
    while bit < peers:
        other = other + bit * lax.rem(lax.rem(me // bit, 2) + lax.rem(k // bit, 2), 2)
        bit *= 2
    return other


def stack_kernel(
    gain, half_taps, capacity, src_slot, row_len, records_ref, ids_ref, tmpl_ref, chan_ref, off_ref, out_ref,
    spread_ref, rows_ref, id_ref, send_buf, recv_buf, visit_buf, unit_ref, table_ref, win_ref, scale_ref, map_ref, map_smem, part_ref, other_ref,
    send_sem, recv_sem, tsend_sem, trecv_sem, csend_sem, crecv_sem, map_sem,
):
    peers = lax.axis_size("tm")
    me, half = lax.axis_index("tm"), lax.axis_index("chan")
    taps = unit_ref.shape[1]
    pair_rows = unit_ref.shape[0] // STOPS
    blocks = scale_ref.shape[1]
    share = other_ref.shape[1]
    position = LANES * lax.broadcasted_iota(jnp.int32, (blocks, LANES), 0) + lax.broadcasted_iota(
        jnp.int32, (blocks, LANES), 1
    )

    group_size = pair_rows // half_taps

    def by_distance(j):
        return peers - 1 - j

    barrier = pltpu.get_barrier_semaphore()

    def greet(k, carry):
        pl.semaphore_signal(
            barrier, inc=1, device_id={"tm": neighbour("tm", k)}, device_id_type=pl.DeviceIdType.MESH
        )
        return carry

    lax.fori_loop(1, peers, greet, 0)
    pl.semaphore_signal(barrier, inc=1, device_id={"chan": 1 - half}, device_id_type=pl.DeviceIdType.MESH)

    def spread(group, carry):
        rows = records_ref[pl.ds(pl.multiple_of(group * 8, 8), 8), :]
        for b in range(blocks):
            spread_ref[pl.ds(b, 8, stride=blocks), :] = rows[:, b * LANES:(b + 1) * LANES]
        for r in range(8):
            rows_ref[group * 8 + r] = spread_ref[r * blocks:(r + 1) * blocks, :]
        return carry

    lax.fori_loop(0, records_ref.shape[0] // 8, spread, 0)
    pl.semaphore_wait(barrier, peers)

    def visit_copy(by):
        return pltpu.make_async_remote_copy(
            src_ref=visit_buf.at[0],
            dst_ref=visit_buf.at[by],
            send_sem=tsend_sem.at[by],
            recv_sem=trecv_sem.at[by],
            device_id={"tm": neighbour("tm", by)},
            device_id_type=pl.DeviceIdType.MESH,
        )

    def rows_copy(k):
        return pltpu.make_async_remote_copy(
            src_ref=send_buf.at[k],
            dst_ref=recv_buf.at[k],
            send_sem=send_sem.at[k],
            recv_sem=recv_sem.at[k],
            device_id={"tm": partner(k)},
            device_id_type=pl.DeviceIdType.MESH,
        )

    def pack(k, buf):
        dest = partner(k)
        for r in range(capacity):
            src = src_slot[dest * capacity + r]
            buf[k, r * blocks:(r + 1) * blocks, :] = jnp.where(position < row_len[src], rows_ref[src], 0.0)
        buf[k, capacity * blocks:, :] = jnp.broadcast_to(ids_ref[pl.ds(dest, 1), :], (8, LANES))

    visit_buf[0, :pair_rows, :] = tmpl_ref[...]
    visit_buf[0, pair_rows:, :] = jnp.zeros((visit_buf.shape[1] - pair_rows, taps), jnp.float32)
    visit_buf[0, pair_rows:pair_rows + group_size, :half_taps] = chan_ref[...].astype(jnp.float32)
    visit_buf[0, pair_rows + group_size:pair_rows + 2 * group_size, :half_taps] = off_ref[...].astype(jnp.float32)
    for by in range(1, STOPS):
        visit_copy(by).start()

    def send_block(j, carry):
        k = by_distance(j)
        pack(k, send_buf)
        rows_copy(k).start()
        return carry

    lax.fori_loop(0, peers - 1, send_block, 0)
    pack(0, recv_buf)

    u_pos = lax.broadcasted_iota(jnp.int32, (LANES, LANES), 0)
    r_pos = lax.broadcasted_iota(jnp.int32, (LANES, LANES), 1)
    lower = u_pos >= r_pos

    def put_table(pair, which, piece):
        around, full = piece[:, :LANES], piece[:, LANES:]
        zero = jnp.zeros_like(around)
        table_ref[pair, which, :LANES, :LANES] = jnp.where(lower, around, zero).astype(jnp.bfloat16)
        table_ref[pair, which, :LANES, LANES:] = zero.astype(jnp.bfloat16)
        table_ref[pair, which, LANES:, :LANES] = full.astype(jnp.bfloat16)
        table_ref[pair, which, LANES:, LANES:] = jnp.where(lower, zero, around).astype(jnp.bfloat16)

    def put_pair(pair):
        row = jnp.broadcast_to(unit_ref[pl.ds(pair, 1), :], (LANES, taps))
        table = pltpu.roll(row, 0, 1, stride=1, stride_axis=0)
        hi = table.astype(jnp.bfloat16).astype(jnp.float32)
        put_table(pair, 0, hi)
        put_table(pair, 1, table - hi)

    back_from = lax.broadcasted_iota(jnp.int32, (taps, taps), 0)
    back_to = lax.broadcasted_iota(jnp.int32, (taps, taps), 1)
    reverse = jnp.where(lax.rem(back_from + back_to, taps) == 0, 1.0, 0.0)

    for by in range(STOPS):
        if by > 0:
            visit_copy(by).wait_recv()
        raw = visit_buf[by, :pair_rows, :]
        centred = raw - jnp.mean(raw, axis=-1, keepdims=True)
        energy = jnp.sum(centred * centred, axis=-1, keepdims=True)
        unit_ref[by * pair_rows:(by + 1) * pair_rows, :] = jnp.dot(
            centred / jnp.sqrt(energy + taps * TEMPLATE_EPS),
            reverse,
            precision=lax.Precision.HIGHEST,
            preferred_element_type=jnp.float32,
        )

        def pair_group(group, carry, by=by):
            for j in range(2):
                put_pair(by * pair_rows + group * 2 + j)
            return carry

        lax.fori_loop(0, pair_rows // 2, pair_group, 0)

    unroll = 4 if capacity % 4 == 0 else 1

    def one_row(k, r):
        x = recv_buf[k, pl.ds(pl.multiple_of(r * blocks, 8), blocks), :]
        win_sum = window_total(x, taps)
        win_sq = window_total(x * x, taps)
        variance = win_sq - win_sum * win_sum / taps
        slot = k * capacity + r
        scale_ref[slot] = gain / jnp.sqrt(jnp.maximum(variance, FLOOR_SHARE * taps))
        hi, lo = split(jnp.concatenate([x, pltpu.roll(x, blocks - 1, 0)], axis=1))
        win_ref[slot, :blocks] = hi
        win_ref[slot, blocks:] = lo

    def rows_of(k):
        def group_of(group, carry):
            for j in range(unroll):
                one_row(k, group * unroll + j)
            return carry

        lax.fori_loop(0, capacity // unroll, group_of, 0)
        id_row = recv_buf[k, capacity * blocks:capacity * blocks + 1, :]
        id_ref[k] = jnp.transpose(jnp.broadcast_to(id_row, (LANES, LANES)))[:id_ref.shape[1]]

    def arrive(j, carry):
        k = by_distance(peers - 2 - j)
        rows_copy(k).wait_recv()
        rows_of(k)
        return carry

    rows_of(0)
    lax.fori_loop(0, peers - 1, arrive, 0)

    id_rows = id_ref.shape[1]
    order = lax.broadcasted_iota(jnp.int32, (id_rows, LANES), 0)
    visit_count = STOPS * group_size
    for row in range(visit_count):
        by, template = divmod(row, group_size)
        at = pair_rows + template
        wanted = visit_buf[by, at:at + 1, :LANES]

        def find(k, found, wanted=wanted):
            number = (order + k * capacity).astype(jnp.float32)
            return jnp.maximum(found, jnp.max(jnp.where(id_ref[k] == wanted, number, 0.0), axis=0, keepdims=True))

        found = lax.fori_loop(0, peers, find, jnp.zeros((1, LANES), jnp.float32), unroll=min(peers, 8))
        map_ref[row:row + 1, :] = jnp.clip(found.astype(jnp.int32), 0, peers * capacity - 1)
        at = at + group_size
        map_ref[visit_count + row:visit_count + row + 1, :] = visit_buf[by, at:at + 1, :LANES].astype(jnp.int32)
    map_copy = pltpu.make_async_copy(map_ref, map_smem, map_sem)
    map_copy.start()
    map_copy.wait()

    lane = lax.broadcasted_iota(jnp.int32, (blocks, LANES), 1)

    def one_pair(row, i):
        pair = row * half_taps + i
        slot = jnp.clip(map_smem[row, i], 0, peers * capacity - 1)
        offset = map_smem[visit_count + row, i]
        windows = win_ref[slot]
        first = jnp.dot(windows, table_ref[pair, 0], preferred_element_type=jnp.float32)
        second = jnp.dot(windows[:blocks], table_ref[pair, 1], preferred_element_type=jnp.float32)
        both = first[:blocks] + first[blocks:] + second
        corr = both[:, :LANES] + pltpu.roll(both[:, LANES:], blocks - 1, 0)
        ratio = corr * scale_ref[slot]
        far = offset >= LANES
        low = jnp.where(far, offset - LANES, offset)
        moved = pltpu.roll(ratio, jnp.where(low == 0, 0, LANES - low), 1)
        below = pltpu.roll(moved, blocks - 1, 0)
        below2 = pltpu.roll(moved, blocks - 2, 0)
        return jnp.where(lane < LANES - low, jnp.where(far, below, moved), jnp.where(far, below2, below))

    def swap(by):
        group = pl.ds(by * group_size, group_size)
        return pltpu.make_async_remote_copy(
            src_ref=part_ref.at[1 - half, group],
            dst_ref=other_ref.at[group],
            send_sem=csend_sem.at[by],
            recv_sem=crecv_sem.at[by],
            device_id={"chan": 1 - half},
            device_id_type=pl.DeviceIdType.MESH,
        )

    for by in range(STOPS):
        def one_template(template, carry, by=by):
            place = by * group_size + template
            total = one_pair(place, 0)
            for i in range(1, half_taps):
                total = total + one_pair(place, i)
            part_ref[0, place] = total[:share]
            part_ref[1, place] = total[share:2 * share]
            return carry

        lax.fori_loop(0, group_size, one_template, 0)
        swap(by).start()

    for by in range(1, STOPS):
        visit_copy(by).wait_send()

    def sent(k, carry):
        rows_copy(k).wait_send()
        return carry

    lax.fori_loop(1, peers, sent, 0)
    for by in range(STOPS):
        swap(by).wait()
        group = pl.ds(by * group_size, group_size)
        stacks = part_ref[half, group] + other_ref[group]
        for b in range(share):
            out_ref[0, by, :, b * LANES:(b + 1) * LANES] = stacks[:, b, :]


def local(records, row_dest, row_chan, row_len, templates, tmpl_chan, tmpl_off):
    slot_count, sample_count = records.shape
    peers = lax.axis_size("tm")
    half_count = lax.axis_size("chan")
    capacity = slot_count // peers
    template_count, half_taps, tap_count = templates.shape
    assert tap_count == 2 * LANES and half_count == 2
    blocks = sample_count // LANES
    lag_count = sample_count - tap_count - MAXOFF
    share = lag_count // LANES // half_count

    slot_ids = jnp.arange(slot_count, dtype=jnp.int32)
    earlier = (row_dest[:, None] == row_dest[None, :]) & (slot_ids[None, :] < slot_ids[:, None])
    rank_within = jnp.sum(earlier.astype(jnp.int32), axis=1)
    target = jnp.where(row_dest >= 0, row_dest * capacity + rank_within, slot_count)
    here = target[None, :] == slot_ids[:, None]
    src_slot = jnp.sum(jnp.where(here, slot_ids[None, :], 0), axis=1)
    ids = jnp.sum(jnp.where(here, row_chan[None, :] + 1, 0), axis=1) - 1
    id_rows = -(-capacity // 8) * 8
    ids = jnp.pad(ids.reshape(peers, capacity), ((0, 0), (0, LANES - capacity)), constant_values=-1)
    ids = ids.astype(jnp.float32)

    pair_rows = template_count * half_taps
    visit_rows = pair_rows + -(-2 * template_count // 8) * 8
    pair_count = STOPS * pair_rows
    gain = math.sqrt(tap_count * half_taps * half_count) / (half_taps * half_count)
    smem = pl.BlockSpec(memory_space=pltpu.SMEM)
    vmem = pl.BlockSpec(memory_space=pltpu.VMEM)
    block_rows = capacity * blocks + 8
    out = pl.pallas_call(
        functools.partial(stack_kernel, gain, half_taps, capacity),
        out_shape=jax.ShapeDtypeStruct((1, STOPS, template_count, share * LANES), jnp.float32),
        in_specs=[smem, smem, vmem, vmem, vmem, vmem, vmem],
        out_specs=vmem,
        scratch_shapes=[
            pltpu.VMEM((8 * blocks, LANES), jnp.float32),
            pltpu.VMEM((slot_count, blocks, LANES), jnp.float32),
            pltpu.VMEM((peers, id_rows, LANES), jnp.float32),
            pltpu.VMEM((peers, block_rows, LANES), jnp.float32),
            pltpu.VMEM((peers, block_rows, LANES), jnp.float32),
            pltpu.VMEM((STOPS, visit_rows, tap_count), jnp.float32),
            pltpu.VMEM((pair_count, tap_count), jnp.float32),
            pltpu.VMEM((pair_count, 2, tap_count, tap_count), jnp.bfloat16),
            pltpu.VMEM((slot_count, 2 * blocks, tap_count), jnp.bfloat16),
            pltpu.VMEM((slot_count, blocks, LANES), jnp.float32),
            pltpu.VMEM((2 * STOPS * template_count, LANES), jnp.int32),
            pltpu.SMEM((2 * STOPS * template_count, LANES), jnp.int32),
            pltpu.VMEM((2, STOPS * template_count, share, LANES), jnp.float32),
            pltpu.VMEM((STOPS * template_count, share, LANES), jnp.float32),
            pltpu.SemaphoreType.DMA((peers,)),
            pltpu.SemaphoreType.DMA((peers,)),
            pltpu.SemaphoreType.DMA((STOPS,)),
            pltpu.SemaphoreType.DMA((STOPS,)),
            pltpu.SemaphoreType.DMA((STOPS,)),
            pltpu.SemaphoreType.DMA((STOPS,)),
            pltpu.SemaphoreType.DMA,
        ],
        compiler_params=pltpu.CompilerParams(
            vmem_limit_bytes=56 * 2**20, collective_id=0, has_side_effects=True
        ),
        cost_estimate=pl.CostEstimate(
            flops=2 * 3 * pair_count * blocks * tap_count * tap_count,
            bytes_accessed=8 * slot_count * sample_count,
            transcendentals=0,
        ),
    )(src_slot, row_len, records, ids, templates.reshape(pair_rows, tap_count), tmpl_chan, tmpl_off)
    return out


def solution(mesh):
    in_specs = (
        P(("fam", "tm", "chan"), None),
        P(("fam", "tm", "chan")),
        P(("fam", "tm", "chan")),
        P(("fam", "tm", "chan")),
        P(("fam", "tm"), "chan", None),
        P(("fam", "tm"), "chan"),
        P(("fam", "tm"), "chan"),
    )
    out_specs = P(("fam", "tm"), None, None, "chan")
    return jax.shard_map(local, mesh=mesh, in_specs=in_specs, out_specs=out_specs, check_vma=False)
```

```python
import functools
import math

import jax
import jax.numpy as jnp
from jax import lax
from jax.experimental import pallas as pl
from jax.experimental.pallas import tpu as pltpu
from jax.sharding import PartitionSpec as P

MAXOFF = 256
STOPS = 4
FLOOR_SHARE = 0.25
TEMPLATE_EPS = 1e-06
LANES = 128


def flat_shift(x, by):
    rows = x.shape[-2]
    if by == LANES:
        return pltpu.roll(x, rows - 1, x.ndim - 2)
    lane = lax.broadcasted_iota(jnp.int32, x.shape, x.ndim - 1)
    moved = pltpu.roll(x, LANES - by, x.ndim - 1)
    below = pltpu.roll(moved, rows - 1, x.ndim - 2)
    return jnp.where(lane < LANES - by, moved, below)


def window_total(x, taps):
    span = 1
    while span < taps:
        x = x + flat_shift(x, span)
        span *= 2
    return x


def split(x):
    hi = x.astype(jnp.bfloat16)
    lo = (x - hi.astype(jnp.float32)).astype(jnp.bfloat16)
    return hi, lo


def neighbour(axis, by):
    return lax.rem(lax.axis_index(axis) + by, lax.axis_size(axis))


def partner(k):
    me, peers = lax.axis_index("tm"), lax.axis_size("tm")
    assert peers & (peers - 1) == 0
    other, bit = 0, 1
    while bit < peers:
        other = other + bit * lax.rem(lax.rem(me // bit, 2) + lax.rem(k // bit, 2), 2)
        bit *= 2
    return other


def stack_kernel(
    gain, half_taps, capacity, src_slot, row_len, records_ref, ids_ref, tmpl_ref, chan_ref, off_ref, out_ref,
    spread_ref, rows_ref, id_ref, send_buf, recv_buf, visit_buf, unit_ref, table_ref, win_ref, scale_ref, map_ref, map_smem, part_ref, other_ref,
    send_sem, recv_sem, tsend_sem, trecv_sem, csend_sem, crecv_sem, map_sem,
):
    peers = lax.axis_size("tm")
    me, half = lax.axis_index("tm"), lax.axis_index("chan")
    taps = unit_ref.shape[1]
    pair_rows = unit_ref.shape[0] // STOPS
    blocks = scale_ref.shape[1]
    share = other_ref.shape[1]
    position = LANES * lax.broadcasted_iota(jnp.int32, (blocks, LANES), 0) + lax.broadcasted_iota(
        jnp.int32, (blocks, LANES), 1
    )

    group_size = pair_rows // half_taps

    def turn(j):
        return half * (peers - 1 - j) + (1 - half) * (j + 1)

    barrier = pltpu.get_barrier_semaphore()

    def greet(k, carry):
        pl.semaphore_signal(
            barrier, inc=1, device_id={"tm": neighbour("tm", k)}, device_id_type=pl.DeviceIdType.MESH
        )
        return carry

    lax.fori_loop(1, peers, greet, 0)
    pl.semaphore_signal(barrier, inc=1, device_id={"chan": 1 - half}, device_id_type=pl.DeviceIdType.MESH)

    def spread(group, carry):
        rows = records_ref[pl.ds(pl.multiple_of(group * 8, 8), 8), :]
        for b in range(blocks):
            spread_ref[pl.ds(b, 8, stride=blocks), :] = rows[:, b * LANES:(b + 1) * LANES]
        for r in range(8):
            rows_ref[group * 8 + r] = spread_ref[r * blocks:(r + 1) * blocks, :]
        return carry

    lax.fori_loop(0, records_ref.shape[0] // 8, spread, 0)
    pl.semaphore_wait(barrier, peers)

    def visit_copy(by):
        return pltpu.make_async_remote_copy(
            src_ref=visit_buf.at[0],
            dst_ref=visit_buf.at[by],
            send_sem=tsend_sem.at[by],
            recv_sem=trecv_sem.at[by],
            device_id={"tm": neighbour("tm", by)},
            device_id_type=pl.DeviceIdType.MESH,
        )

    def rows_copy(k):
        return pltpu.make_async_remote_copy(
            src_ref=send_buf.at[k],
            dst_ref=recv_buf.at[k],
            send_sem=send_sem.at[k],
            recv_sem=recv_sem.at[k],
            device_id={"tm": partner(k)},
            device_id_type=pl.DeviceIdType.MESH,
        )

    def pack(k, buf):
        dest = partner(k)
        for r in range(capacity):
            src = src_slot[dest * capacity + r]
            buf[k, r * blocks:(r + 1) * blocks, :] = jnp.where(position < row_len[src], rows_ref[src], 0.0)
        buf[k, capacity * blocks:, :] = jnp.broadcast_to(ids_ref[pl.ds(dest, 1), :], (8, LANES))

    visit_buf[0, :pair_rows, :] = tmpl_ref[...]
    visit_buf[0, pair_rows:, :] = jnp.zeros((visit_buf.shape[1] - pair_rows, taps), jnp.float32)
    visit_buf[0, pair_rows:pair_rows + group_size, :half_taps] = chan_ref[...].astype(jnp.float32)
    visit_buf[0, pair_rows + group_size:pair_rows + 2 * group_size, :half_taps] = off_ref[...].astype(jnp.float32)
    for by in range(1, STOPS):
        visit_copy(by).start()

    def send_block(j, carry):
        k = turn(j)
        pack(k, send_buf)
        rows_copy(k).start()
        return carry

    lax.fori_loop(0, peers - 1, send_block, 0)
    pack(0, recv_buf)

    u_pos = lax.broadcasted_iota(jnp.int32, (LANES, LANES), 0)
    r_pos = lax.broadcasted_iota(jnp.int32, (LANES, LANES), 1)
    lower = u_pos >= r_pos

    def put_table(pair, which, piece):
        around, full = piece[:, :LANES], piece[:, LANES:]
        zero = jnp.zeros_like(around)
        table_ref[pair, which, :LANES, :LANES] = jnp.where(lower, around, zero).astype(jnp.bfloat16)
        table_ref[pair, which, :LANES, LANES:] = zero.astype(jnp.bfloat16)
        table_ref[pair, which, LANES:, :LANES] = full.astype(jnp.bfloat16)
        table_ref[pair, which, LANES:, LANES:] = jnp.where(lower, zero, around).astype(jnp.bfloat16)

    def put_pair(pair):
        row = jnp.broadcast_to(unit_ref[pl.ds(pair, 1), :], (LANES, taps))
        table = pltpu.roll(row, 0, 1, stride=1, stride_axis=0)
        hi = table.astype(jnp.bfloat16).astype(jnp.float32)
        put_table(pair, 0, hi)
        put_table(pair, 1, table - hi)

    back_from = lax.broadcasted_iota(jnp.int32, (taps, taps), 0)
    back_to = lax.broadcasted_iota(jnp.int32, (taps, taps), 1)
    reverse = jnp.where(lax.rem(back_from + back_to, taps) == 0, 1.0, 0.0)

    for by in range(STOPS):
        if by > 0:
            visit_copy(by).wait_recv()
        raw = visit_buf[by, :pair_rows, :]
        centred = raw - jnp.mean(raw, axis=-1, keepdims=True)
        energy = jnp.sum(centred * centred, axis=-1, keepdims=True)
        unit_ref[by * pair_rows:(by + 1) * pair_rows, :] = jnp.dot(
            centred / jnp.sqrt(energy + taps * TEMPLATE_EPS),
            reverse,
            precision=lax.Precision.HIGHEST,
            preferred_element_type=jnp.float32,
        )

        def pair_group(group, carry, by=by):
            for j in range(2):
                put_pair(by * pair_rows + group * 2 + j)
            return carry

        lax.fori_loop(0, pair_rows // 2, pair_group, 0)

    unroll = 4 if capacity % 4 == 0 else 1

    def one_row(k, r):
        x = recv_buf[k, pl.ds(pl.multiple_of(r * blocks, 8), blocks), :]
        win_sum = window_total(x, taps)
        win_sq = window_total(x * x, taps)
        variance = win_sq - win_sum * win_sum / taps
        slot = k * capacity + r
        scale_ref[slot] = gain / jnp.sqrt(jnp.maximum(variance, FLOOR_SHARE * taps))
        hi, lo = split(jnp.concatenate([x, pltpu.roll(x, blocks - 1, 0)], axis=1))
        win_ref[slot, :blocks] = hi
        win_ref[slot, blocks:] = lo

    def rows_of(k):
        def group_of(group, carry):
            for j in range(unroll):
                one_row(k, group * unroll + j)
            return carry

        lax.fori_loop(0, capacity // unroll, group_of, 0)
        id_row = recv_buf[k, capacity * blocks:capacity * blocks + 1, :]
        id_ref[k] = jnp.transpose(jnp.broadcast_to(id_row, (LANES, LANES)))[:id_ref.shape[1]]

    def arrive(j, carry):
        k = turn(j)
        rows_copy(k).wait_recv()
        rows_of(k)
        return carry

    rows_of(0)
    lax.fori_loop(0, peers - 1, arrive, 0)

    id_rows = id_ref.shape[1]
    order = lax.broadcasted_iota(jnp.int32, (id_rows, LANES), 0)
    visit_count = STOPS * group_size
    for row in range(visit_count):
        by, template = divmod(row, group_size)
        at = pair_rows + template
        wanted = visit_buf[by, at:at + 1, :LANES]

        def find(k, found, wanted=wanted):
            number = (order + k * capacity).astype(jnp.float32)
            return jnp.maximum(found, jnp.max(jnp.where(id_ref[k] == wanted, number, 0.0), axis=0, keepdims=True))

        found = lax.fori_loop(0, peers, find, jnp.zeros((1, LANES), jnp.float32), unroll=min(peers, 8))
        map_ref[row:row + 1, :] = jnp.clip(found.astype(jnp.int32), 0, peers * capacity - 1)
        at = at + group_size
        map_ref[visit_count + row:visit_count + row + 1, :] = visit_buf[by, at:at + 1, :LANES].astype(jnp.int32)
    map_copy = pltpu.make_async_copy(map_ref, map_smem, map_sem)
    map_copy.start()
    map_copy.wait()

    lane = lax.broadcasted_iota(jnp.int32, (blocks, LANES), 1)

    def one_pair(row, i):
        pair = row * half_taps + i
        slot = jnp.clip(map_smem[row, i], 0, peers * capacity - 1)
        offset = map_smem[visit_count + row, i]
        windows = win_ref[slot]
        first = jnp.dot(windows, table_ref[pair, 0], preferred_element_type=jnp.float32)
        second = jnp.dot(windows[:blocks], table_ref[pair, 1], preferred_element_type=jnp.float32)
        both = first[:blocks] + first[blocks:] + second
        corr = both[:, :LANES] + pltpu.roll(both[:, LANES:], blocks - 1, 0)
        ratio = corr * scale_ref[slot]
        far = offset >= LANES
        low = jnp.where(far, offset - LANES, offset)
        moved = pltpu.roll(ratio, jnp.where(low == 0, 0, LANES - low), 1)
        below = pltpu.roll(moved, blocks - 1, 0)
        below2 = pltpu.roll(moved, blocks - 2, 0)
        return jnp.where(lane < LANES - low, jnp.where(far, below, moved), jnp.where(far, below2, below))

    def swap(by):
        group = pl.ds(by * group_size, group_size)
        return pltpu.make_async_remote_copy(
            src_ref=part_ref.at[1 - half, group],
            dst_ref=other_ref.at[group],
            send_sem=csend_sem.at[by],
            recv_sem=crecv_sem.at[by],
            device_id={"chan": 1 - half},
            device_id_type=pl.DeviceIdType.MESH,
        )

    for by in range(STOPS):
        def one_template(template, carry, by=by):
            place = by * group_size + template
            total = one_pair(place, 0)
            for i in range(1, half_taps):
                total = total + one_pair(place, i)
            part_ref[0, place] = total[:share]
            part_ref[1, place] = total[share:2 * share]
            return carry

        lax.fori_loop(0, group_size, one_template, 0)
        swap(by).start()

    for by in range(1, STOPS):
        visit_copy(by).wait_send()

    def sent(k, carry):
        rows_copy(k).wait_send()
        return carry

    lax.fori_loop(1, peers, sent, 0)
    for by in range(STOPS):
        swap(by).wait()
        group = pl.ds(by * group_size, group_size)
        stacks = part_ref[half, group] + other_ref[group]
        for b in range(share):
            out_ref[0, by, :, b * LANES:(b + 1) * LANES] = stacks[:, b, :]


def local(records, row_dest, row_chan, row_len, templates, tmpl_chan, tmpl_off):
    slot_count, sample_count = records.shape
    peers = lax.axis_size("tm")
    half_count = lax.axis_size("chan")
    capacity = slot_count // peers
    template_count, half_taps, tap_count = templates.shape
    assert tap_count == 2 * LANES and half_count == 2
    blocks = sample_count // LANES
    lag_count = sample_count - tap_count - MAXOFF
    share = lag_count // LANES // half_count

    slot_ids = jnp.arange(slot_count, dtype=jnp.int32)
    earlier = (row_dest[:, None] == row_dest[None, :]) & (slot_ids[None, :] < slot_ids[:, None])
    rank_within = jnp.sum(earlier.astype(jnp.int32), axis=1)
    target = jnp.where(row_dest >= 0, row_dest * capacity + rank_within, slot_count)
    here = target[None, :] == slot_ids[:, None]
    src_slot = jnp.sum(jnp.where(here, slot_ids[None, :], 0), axis=1)
    ids = jnp.sum(jnp.where(here, row_chan[None, :] + 1, 0), axis=1) - 1
    id_rows = -(-capacity // 8) * 8
    ids = jnp.pad(ids.reshape(peers, capacity), ((0, 0), (0, LANES - capacity)), constant_values=-1)
    ids = ids.astype(jnp.float32)

    pair_rows = template_count * half_taps
    visit_rows = pair_rows + -(-2 * template_count // 8) * 8
    pair_count = STOPS * pair_rows
    gain = math.sqrt(tap_count * half_taps * half_count) / (half_taps * half_count)
    smem = pl.BlockSpec(memory_space=pltpu.SMEM)
    vmem = pl.BlockSpec(memory_space=pltpu.VMEM)
    block_rows = capacity * blocks + 8
    out = pl.pallas_call(
        functools.partial(stack_kernel, gain, half_taps, capacity),
        out_shape=jax.ShapeDtypeStruct((1, STOPS, template_count, share * LANES), jnp.float32),
        in_specs=[smem, smem, vmem, vmem, vmem, vmem, vmem],
        out_specs=vmem,
        scratch_shapes=[
            pltpu.VMEM((8 * blocks, LANES), jnp.float32),
            pltpu.VMEM((slot_count, blocks, LANES), jnp.float32),
            pltpu.VMEM((peers, id_rows, LANES), jnp.float32),
            pltpu.VMEM((peers, block_rows, LANES), jnp.float32),
            pltpu.VMEM((peers, block_rows, LANES), jnp.float32),
            pltpu.VMEM((STOPS, visit_rows, tap_count), jnp.float32),
            pltpu.VMEM((pair_count, tap_count), jnp.float32),
            pltpu.VMEM((pair_count, 2, tap_count, tap_count), jnp.bfloat16),
            pltpu.VMEM((slot_count, 2 * blocks, tap_count), jnp.bfloat16),
            pltpu.VMEM((slot_count, blocks, LANES), jnp.float32),
            pltpu.VMEM((2 * STOPS * template_count, LANES), jnp.int32),
            pltpu.SMEM((2 * STOPS * template_count, LANES), jnp.int32),
            pltpu.VMEM((2, STOPS * template_count, share, LANES), jnp.float32),
            pltpu.VMEM((STOPS * template_count, share, LANES), jnp.float32),
            pltpu.SemaphoreType.DMA((peers,)),
            pltpu.SemaphoreType.DMA((peers,)),
            pltpu.SemaphoreType.DMA((STOPS,)),
            pltpu.SemaphoreType.DMA((STOPS,)),
            pltpu.SemaphoreType.DMA((STOPS,)),
            pltpu.SemaphoreType.DMA((STOPS,)),
            pltpu.SemaphoreType.DMA,
        ],
        compiler_params=pltpu.CompilerParams(
            vmem_limit_bytes=56 * 2**20, collective_id=0, has_side_effects=True
        ),
        cost_estimate=pl.CostEstimate(
            flops=2 * 3 * pair_count * blocks * tap_count * tap_count,
            bytes_accessed=8 * slot_count * sample_count,
            transcendentals=0,
        ),
    )(src_slot, row_len, records, ids, templates.reshape(pair_rows, tap_count), tmpl_chan, tmpl_off)
    return out


def solution(mesh):
    in_specs = (
        P(("fam", "tm", "chan"), None),
        P(("fam", "tm", "chan")),
        P(("fam", "tm", "chan")),
        P(("fam", "tm", "chan")),
        P(("fam", "tm"), "chan", None),
        P(("fam", "tm"), "chan"),
        P(("fam", "tm"), "chan"),
    )
    out_specs = P(("fam", "tm"), None, None, "chan")
    return jax.shard_map(local, mesh=mesh, in_specs=in_specs, out_specs=out_specs, check_vma=False)
```
